32 devices in a mesh: slab: 8 (over y, x, core), lat: 4 (over z).
Axes of the slice: x: 2, y: 2, z: 4, core: 2. Of those that a mesh axis runs over, the one named last changes fastest.
Arguments:
- nodes: bfloat16 [4096, 512], P('slab', 'lat')
- edges: bfloat16 [16384, 512], P(('slab', 'lat'))
- edge_tiles: int32 [2, 128], P(None, ('slab', 'lat')), may hold values from 0 to 7, as said below
- edge_offsets: int32 [2, 16384], P(None, ('slab', 'lat')), may hold values from 0 to 127
- tile_counts: int32 [8], P('slab'), may hold values from 5 to 16, as said below
- halo_blocks: int32 [8, 2, 2], P('slab'), may hold values from 0 to 3
- w_edge_in: bfloat16 [1536, 512], P(('slab', 'lat')), may hold values from -0.15625 to 0.15625
- w_edge_out: bfloat16 [512, 512], P(('slab', 'lat'))
- w_node_in: bfloat16 [1024, 512], P(('slab', 'lat')), may hold values from -0.1875 to 0.1875
- w_node_out: bfloat16 [512, 512], P(('slab', 'lat'))
- edge_gain: float32 [512], replicated, may hold values from 0.1 to 1.9
- node_gain: float32 [512], replicated, may hold values from 0.1 to 1.9
- node_cotangent: bfloat16 [4096, 512], P('slab', 'lat'), may hold values from -6 to 6
- edge_cotangent: bfloat16 [16384, 512], P(('slab', 'lat')), may hold values from -6 to 6
Outputs:
- new_nodes: bfloat16 [4096, 512], P('slab', 'lat')
- new_edges: bfloat16 [16384, 512], P(('slab', 'lat'))
- grad_nodes: bfloat16 [4096, 512], P('slab', 'lat')
- grad_edges: bfloat16 [16384, 512], P(('slab', 'lat'))
- grad_edge_in: float32 [1536, 512], P(('slab', 'lat'))
- grad_edge_out: float32 [512, 512], P(('slab', 'lat'))
- grad_node_in: float32 [1024, 512], P(('slab', 'lat'))
- grad_node_out: float32 [512, 512], P(('slab', 'lat'))
The draws below stay inside these ranges and needn't reach their ends.
Inputs may be any that keep to these rules, and one draw needn't show every extreme that they name: `edge_tiles`: row 0 names each tile's receiver block among its slab's 4 blocks; row 1 its sender block among the 8 blocks of the extended slab (2 received from below, the slab's own, 2 received from above). Tiles of the first slab never name the blocks from below, tiles of the last slab never those from above. `tile_counts`: live tiles are the first ones of the slab's 16 slots; in every draw some slab has all slots live.
All inputs are finite; a program needn't handle non-finite values.
Results may differ from the reference program's by a relative error of at most 0.03.
The reference program's roundings to bfloat16 on the way count: a program that leaves them out, or rounds other values in their place, can miss the bound.
Values may be sent and summed in bfloat16 or wider, within the bound.
A program may use at most 64 MiB of HBM per device.

```python
import math
import jax
import jax.numpy as jnp
from jax import lax

L = 512
HID = 512
BLK = 128
HB = 2
NB_SLAB = 4
XB = 8
TILES_SLAB = 16
TILES = 128
EDGES = 16384
NODES = 4096
N_SLAB = 8


def row_scaled(key, row_count, col_count):
    first_key, second_key = jax.random.split(key, 2)
    row_scale = jnp.exp(jax.random.uniform(second_key, (row_count, 1), jnp.float32, math.log(0.3), math.log(3.0)))
    return jax.random.normal(first_key, (row_count, col_count), jnp.float32) * row_scale


def column_scaled(key, row_count, col_count):
    first_key, second_key = jax.random.split(key, 2)
    col_scale = jnp.exp(jax.random.uniform(second_key, (1, col_count), jnp.float32, math.log(0.3), math.log(3.0)))
    base = jax.random.normal(first_key, (row_count, col_count), jnp.float32)
    return base * col_scale / math.sqrt(row_count)


def draw_nodes(key, part):
    return row_scaled(jax.random.fold_in(key, 11), NODES, L).astype(jnp.bfloat16)


def draw_edges(key, part):
    return row_scaled(jax.random.fold_in(key, 12), EDGES, L).astype(jnp.bfloat16)


def draw_w_edge_out(key, part):
    return column_scaled(jax.random.fold_in(key, 13), HID, L).astype(jnp.bfloat16)


def draw_w_node_out(key, part):
    return column_scaled(jax.random.fold_in(key, 14), HID, L).astype(jnp.bfloat16)


def draw_edge_tiles(key, part):
    first_key, second_key = jax.random.split(jax.random.fold_in(key, 21), 2)
    slab_of = jnp.arange(TILES, dtype=jnp.int32) // TILES_SLAB
    receiver = jax.random.randint(first_key, (TILES,), 0, NB_SLAB, dtype=jnp.int32)
    lowest = jnp.where(slab_of == 0, HB, 0).astype(jnp.int32)
    highest = jnp.where(slab_of == N_SLAB - 1, HB + NB_SLAB, XB).astype(jnp.int32)
    sender = jax.random.randint(second_key, (TILES,), lowest, highest, dtype=jnp.int32)
    return jnp.stack([receiver, sender]).astype(jnp.int32)


def draw_tile_counts(key, part):
    first_key, second_key = jax.random.split(jax.random.fold_in(key, 31), 2)
    counts = jax.random.randint(first_key, (N_SLAB,), TILES_SLAB // 3, TILES_SLAB + 1, dtype=jnp.int32)
    chosen = jax.random.randint(second_key, (), 0, N_SLAB, dtype=jnp.int32)
    return counts.at[chosen].set(TILES_SLAB).astype(jnp.int32)


def with_ends(values, own_key, low, largest):
    longest = values.shape.index(max(values.shape))
    spots = []
    for shift in (0, 1):
        where = [jax.random.randint(jax.random.fold_in(own_key, axis), (), 0, length) for axis, length in enumerate(values.shape)]
        where[longest] = (where[longest] + shift) % values.shape[longest]
        spots.append(tuple(where))
    return values.at[spots[0]].set(low).at[spots[1]].set(largest)


def levels(key, shape, cuts, least, largest):
    def one(position, shards_of):
        steps = jax.random.uniform(jax.random.fold_in(jax.random.fold_in(key, 6), position), (shards_of,), jnp.float32, least / len(cuts), largest / len(cuts))
        return jnp.repeat(jnp.exp(steps), shape[position] // shards_of).reshape((-1,) + (1,) * (len(shape) - position - 1))

    loudness = one(*cuts[0])
    for cut in cuts[1:]:
        loudness = loudness * one(*cut)
    return loudness


def normal_values(stream_key, extent, scale, reach, shards=(), held_as=jnp.bfloat16):
    loudness = levels(stream_key, extent, shards, -0.22, 0.18) if shards else 1.0
    array = jax.random.normal(stream_key, extent, jnp.float32) * scale * loudness
    return jnp.minimum(jnp.maximum(array, -reach), reach).astype(held_as)


def setup_inputs(seed: int = 0) -> dict:
    splits = jax.random.split(jax.random.key(seed), 15)
    return {
        "nodes": draw_nodes(jax.random.fold_in(splits[14], 71), 0),
        "edges": draw_edges(jax.random.fold_in(splits[14], 71), 0),
        "edge_tiles": draw_edge_tiles(jax.random.fold_in(splits[14], 71), 0),
        "edge_offsets": with_ends(jax.random.randint(splits[3], (2, EDGES), 0, BLK), jax.random.fold_in(splits[3], 1), 0, BLK - 1).astype(jnp.int32),
        "tile_counts": draw_tile_counts(jax.random.fold_in(splits[14], 71), 0),
        "halo_blocks": with_ends(jax.random.randint(splits[5], (N_SLAB, 2, HB), 0, NB_SLAB), jax.random.fold_in(splits[5], 1), 0, NB_SLAB - 1).astype(jnp.int32),
        "w_edge_in": normal_values(splits[6], (3 * L, HID), (3 * L) ** -0.5, 0.15625, ((0, 32),)),
        "w_edge_out": draw_w_edge_out(jax.random.fold_in(splits[14], 71), 0),
        "w_node_in": normal_values(splits[8], (2 * L, HID), (2 * L) ** -0.5, 0.1875, ((0, 32),)),
        "w_node_out": draw_w_node_out(jax.random.fold_in(splits[14], 71), 0),
        "edge_gain": jnp.clip(1.0 + 0.18 * jax.random.normal(splits[10], (L,), jnp.float32), 0.1, 1.9),
        "node_gain": jnp.clip(1.0 + 0.18 * jax.random.normal(splits[11], (L,), jnp.float32), 0.1, 1.9),
        "node_cotangent": normal_values(splits[12], (NODES, L), 1.0, 6.0, ((0, 8), (1, 4))),
        "edge_cotangent": normal_values(splits[13], (EDGES, L), 1.0, 6.0, ((0, 32),)),
    }


EPSILON = 1e-05

def layer_norm(values, gain_vector):
    average = lax.optimization_barrier(jnp.mean(values, axis=-1, keepdims=True))
    centred = values - average
    variance = lax.optimization_barrier(jnp.mean(centred * centred, axis=-1, keepdims=True))
    inverse = lax.rsqrt(variance + EPSILON)
    normed = centred * inverse
    return (normed * gain_vector, normed, inverse)

def norm_back(upstream, normed, inverse, gain_vector):
    scaled = upstream * gain_vector
    return inverse * (scaled - lax.optimization_barrier(jnp.mean(scaled, axis=-1, keepdims=True)) - normed * lax.optimization_barrier(jnp.mean(scaled * normed, axis=-1, keepdims=True)))

def contract_rows(left, right):
    return lax.dot_general(left, right, (((0,), (0,)), ((), ())), preferred_element_type=jnp.float32)

def times_transpose(left, weight):
    return lax.dot_general(left, weight, (((1,), (1,)), ((), ())), preferred_element_type=jnp.float32)

def pick_blocks(source_table, blocks):
    width = source_table.shape[1]
    return jnp.take(source_table.reshape(-1, BLK, width), blocks, axis=0).reshape(-1, width)

def add_blocks(source_table, blocks, values):
    width = source_table.shape[1]
    shaped = source_table.reshape(-1, BLK, width).at[blocks].add(values.reshape(-1, BLK, width))
    return shaped.reshape(-1, width)

def reference(nodes, edges, edge_tiles, edge_offsets, tile_counts, halo_blocks, w_edge_in, w_edge_out, w_node_in, w_node_out, edge_gain, node_gain, node_cotangent, edge_cotangent):
    slab_rows = NB_SLAB * BLK
    halo_rows = HB * BLK
    slab_edges = TILES_SLAB * BLK
    latents = nodes.reshape(N_SLAB, slab_rows, L)
    to_upper = jax.vmap(pick_blocks)(latents, halo_blocks[:, 0])
    to_lower = jax.vmap(pick_blocks)(latents, halo_blocks[:, 1])
    blank_rows = jnp.zeros((1, halo_rows, L), nodes.dtype)
    from_lower = jnp.concatenate([blank_rows, to_upper[:-1]], axis=0)
    from_upper = jnp.concatenate([to_lower[1:], blank_rows], axis=0)
    extended_all = jnp.concatenate([from_lower, latents, from_upper], axis=1)
    slab_tiles = edge_tiles.reshape(2, N_SLAB, TILES_SLAB).transpose(1, 0, 2)
    slab_offsets = edge_offsets.reshape(2, N_SLAB, slab_edges).transpose(1, 0, 2)
    slab_edge_latents = edges.reshape(N_SLAB, slab_edges, L)
    slab_node_cot = node_cotangent.reshape(N_SLAB, slab_rows, L)
    slab_edge_cot = edge_cotangent.reshape(N_SLAB, slab_edges, L)

    def one_slab(totals, inputs):
        extended, tiles, offsets, count, edge_latents, node_cot, edge_cot = inputs
        slab_full = extended[halo_rows:halo_rows + slab_rows]
        tile_of = jnp.arange(slab_edges, dtype=jnp.int32) // BLK
        dst_row = tiles[0][tile_of] * BLK + offsets[0]
        src_row = tiles[1][tile_of] * BLK + offsets[1]
        live_mask = (tile_of < count).astype(jnp.float32)[:, None]
        joined = jnp.concatenate([edge_latents, extended[src_row], slab_full[dst_row]], axis=1)
        edge_first = jax.nn.relu(jnp.dot(joined, w_edge_in, preferred_element_type=jnp.float32)).astype(jnp.bfloat16)
        edge_second = jnp.dot(edge_first, w_edge_out, preferred_element_type=jnp.float32)
        edge_update, edge_normed, edge_inverse = layer_norm(edge_second, edge_gain)
        message = edge_update * live_mask
        new_edge_rows = (edge_latents.astype(jnp.float32) + message).astype(jnp.bfloat16)
        summed = jnp.zeros((slab_rows, L), jnp.float32).at[dst_row].add(message)
        aggregated = summed.astype(jnp.bfloat16)
        node_joined = jnp.concatenate([slab_full, aggregated], axis=1)
        node_first = jax.nn.relu(jnp.dot(node_joined, w_node_in, preferred_element_type=jnp.float32)).astype(jnp.bfloat16)
        node_second = jnp.dot(node_first, w_node_out, preferred_element_type=jnp.float32)
        node_update, node_normed, node_inverse = layer_norm(node_second, node_gain)
        new_rows = (slab_full.astype(jnp.float32) + node_update).astype(jnp.bfloat16)
        d_node_second = norm_back(node_cot.astype(jnp.float32), node_normed, node_inverse, node_gain).astype(jnp.bfloat16)
        g_node_out = contract_rows(node_first, d_node_second)
        d_node_first = (times_transpose(d_node_second, w_node_out) * (node_first > 0)).astype(jnp.bfloat16)
        g_node_in = contract_rows(node_joined, d_node_first)
        d_node_joined = times_transpose(d_node_first, w_node_in)
        d_direct = d_node_joined[:, :L]
        d_aggregated = d_node_joined[:, L:].astype(jnp.bfloat16)
        edge_upstream = edge_cot.astype(jnp.float32)
        d_message = (edge_upstream + d_aggregated[dst_row].astype(jnp.float32)) * live_mask
        d_edge_second = norm_back(d_message, edge_normed, edge_inverse, edge_gain).astype(jnp.bfloat16)
        g_edge_out = contract_rows(edge_first, d_edge_second)
        d_edge_first = (times_transpose(d_edge_second, w_edge_out) * (edge_first > 0)).astype(jnp.bfloat16)
        g_edge_in = contract_rows(joined, d_edge_first)
        d_joined = times_transpose(d_edge_first, w_edge_in)
        grad_edge_rows = (edge_upstream + d_joined[:, :L]).astype(jnp.bfloat16)
        d_extended = jnp.zeros((XB * BLK, L), jnp.float32)
        d_extended = d_extended.at[src_row].add(d_joined[:, L:2 * L])
        d_extended = d_extended.at[halo_rows + dst_row].add(d_joined[:, 2 * L:])
        d_extended = d_extended.at[halo_rows:halo_rows + slab_rows].add(d_direct)
        totals = (totals[0] + g_edge_in, totals[1] + g_edge_out, totals[2] + g_node_in, totals[3] + g_node_out)
        return (totals, (new_rows, new_edge_rows, grad_edge_rows, d_extended))
    start_totals = (jnp.zeros((3 * L, HID), jnp.float32), jnp.zeros((HID, L), jnp.float32), jnp.zeros((2 * L, HID), jnp.float32), jnp.zeros((HID, L), jnp.float32))
    totals, outputs = lax.scan(one_slab, start_totals, (extended_all, slab_tiles, slab_offsets, tile_counts, slab_edge_latents, slab_node_cot, slab_edge_cot))
    new_rows, new_edge_rows, grad_edge_rows, d_extended = outputs
    d_lower = d_extended[:, :halo_rows]
    d_middle = d_extended[:, halo_rows:halo_rows + slab_rows]
    d_upper = d_extended[:, halo_rows + slab_rows:]
    blank_grad = jnp.zeros((1, halo_rows, L), jnp.float32)
    from_above = jnp.concatenate([d_lower[1:], blank_grad], axis=0)
    from_below = jnp.concatenate([blank_grad, d_upper[:-1]], axis=0)
    grad_slabs = jax.vmap(add_blocks)(d_middle, halo_blocks[:, 0], from_above)
    grad_slabs = jax.vmap(add_blocks)(grad_slabs, halo_blocks[:, 1], from_below)
    return (new_rows.reshape(NODES, L), new_edge_rows.reshape(EDGES, L), grad_slabs.astype(jnp.bfloat16).reshape(NODES, L), grad_edge_rows.reshape(EDGES, L), totals[0], totals[1], totals[2], totals[3])
```

```python
import functools

import jax
import jax.numpy as jnp
from jax import lax
from jax.experimental import pallas as pl
from jax.experimental.pallas import tpu as pltpu
from jax.sharding import PartitionSpec as P

L = 512
BLK = 128
HB = 2


EPSILON = 1e-05

MESH = pl.DeviceIdType.MESH
GROUP_OF = (0, 1, 1, 1)


def bits_of(count):
    return count.bit_length() - 1


def bit_at(index, b):
    return lax.rem(lax.div(index, 1 << b), 2)


def partner(axis, b):
    index = lax.axis_index(axis)
    return {axis: index + (1 - 2 * bit_at(index, b)) * (1 << b)}


def greet(slab_bits, lat_bits):
    barrier = pltpu.get_barrier_semaphore()
    for axis, count in (("slab", slab_bits), ("lat", lat_bits)):
        for b in range(count):
            pl.semaphore_signal(barrier, inc=1, device_id=partner(axis, b), device_id_type=MESH)
    pl.semaphore_wait(barrier, slab_bits + lat_bits)


def slab_order(slab_bits, group):
    rest = list(range(1, slab_bits))
    return [0] + (rest if group == 0 else rest[::-1])


def gather_kernel(slab_bits, lat_bits, *refs):
    shards, fulls = refs[:4], refs[4:8]
    send_sem, recv_sem = refs[8:]
    slab, lat = lax.axis_index("slab"), lax.axis_index("lat")
    slab_at = [bit_at(slab, b) for b in range(slab_bits)]
    greet(slab_bits, lat_bits)
    for shard, full in zip(shards, fulls):
        spot = tuple(slab_at[::-1]) + (lat,)
        full[spot] = shard[...]
    steps = slab_bits + lat_bits

    def start(i, step):
        full = fulls[i]
        order = slab_order(slab_bits, GROUP_OF[i])[::-1]
        if step < lat_bits:
            size = 1 << step
            rows = pl.ds(lax.div(lat, size) * size, size)
            spot = tuple(slab_at[::-1]) + (rows,)
            to = partner("lat", step)
        else:
            done = order[: step - lat_bits]
            spot = tuple(
                slice(None) if b in done else slab_at[b] for b in reversed(range(slab_bits))
            )
            to = partner("slab", order[step - lat_bits])
        copy = pltpu.make_async_remote_copy(
            src_ref=full.at[spot],
            dst_ref=full.at[spot],
            send_sem=send_sem.at[i, step],
            recv_sem=recv_sem.at[i, step],
            device_id=to,
            device_id_type=MESH,
        )
        copy.start()
        return copy

    copies = [[start(i, 0)] for i in range(4)]
    for step in range(steps):
        for i in range(4):
            copies[i][step].wait_recv()
            if step + 1 < steps:
                copies[i].append(start(i, step + 1))
    for row in copies:
        for copy in row:
            copy.wait_send()


def gather_weights(shards, slab_count, lat_count):
    slab_bits, lat_bits = bits_of(slab_count), bits_of(lat_count)
    steps = slab_bits + lat_bits
    fulls = pl.pallas_call(
        functools.partial(gather_kernel, slab_bits, lat_bits),
        out_shape=[
            jax.ShapeDtypeStruct((2,) * slab_bits + (lat_count,) + w.shape, w.dtype) for w in shards
        ],
        in_specs=[pl.BlockSpec(memory_space=pltpu.VMEM)] * 4,
        out_specs=[pl.BlockSpec(memory_space=pltpu.VMEM)] * 4,
        scratch_shapes=[
            pltpu.SemaphoreType.DMA((4, steps)),
            pltpu.SemaphoreType.DMA((4, steps)),
        ],
        compiler_params=pltpu.CompilerParams(
            collective_id=0, has_side_effects=True, vmem_limit_bytes=40 * 1024 * 1024
        ),
        name="gather_weights",
    )(*shards)
    return [full.reshape(-1, full.shape[-1]) for full in fulls]


def sum_shapes(slab_bits, lat_count, rows, width):
    shapes = [(2,) * (slab_bits - 1 - k) + (lat_count, rows, width) for k in range(slab_bits)]
    while lat_count > 1:
        lat_count //= 2
        shapes.append((lat_count, rows, width))
    return shapes


def scatter_kernel(slab_bits, lat_bits, *refs):
    steps = slab_bits + lat_bits
    parts, outs = refs[:4], refs[4:8]
    got = [refs[8 + i * steps : 8 + (i + 1) * steps] for i in range(4)]
    refs = refs[8 + 4 * steps :]
    held = [refs[i * (steps - 1) : (i + 1) * (steps - 1)] for i in range(4)]
    send_sem, recv_sem = refs[4 * (steps - 1) :]
    slab, lat = lax.axis_index("slab"), lax.axis_index("lat")
    greet(slab_bits, lat_bits)

    def plan(i, step):
        if step < slab_bits:
            order = slab_order(slab_bits, GROUP_OF[i])
            b = order[step]
            left = sorted(set(range(slab_bits)) - set(order[:step]), reverse=True)
            lead = (slice(None),) * left.index(b)
            mine = bit_at(slab, b)
            return lead + (mine,), lead + (1 - mine,), partner("slab", b)
        b = lat_bits - 1 - (step - slab_bits)
        size = 1 << b
        mine = bit_at(lat, b)
        return (pl.ds(mine * size, size),), (pl.ds((1 - mine) * size, size),), partner("lat", b)

    def source(i, step):
        return parts[i] if step == 0 else held[i][step - 1]

    def start(i, step):
        _, theirs, to = plan(i, step)
        copy = pltpu.make_async_remote_copy(
            src_ref=source(i, step).at[theirs],
            dst_ref=got[i][step],
            send_sem=send_sem.at[i, step],
            recv_sem=recv_sem.at[i, step],
            device_id=to,
            device_id_type=MESH,
        )
        copy.start()
        return copy

    copies = [[start(i, 0)] for i in range(4)]
    for step in range(steps):
        for i in range(4):
            copies[i][step].wait_recv()
            mine, _, _ = plan(i, step)
            total = source(i, step)[mine].astype(jnp.float32) + got[i][step][...].astype(jnp.float32)
            if step + 1 < steps:
                held[i][step][...] = total.astype(jnp.bfloat16)
                copies[i].append(start(i, step + 1))
            else:
                outs[i][...] = total.reshape(outs[i].shape)
    for row in copies:
        for copy in row:
            copy.wait_send()


def scatter_grads(grads, slab_count, lat_count):
    slab_bits, lat_bits = bits_of(slab_count), bits_of(lat_count)
    steps = slab_bits + lat_bits
    shards = slab_count * lat_count
    width = grads[0].shape[1]
    shapes = [sum_shapes(slab_bits, lat_count, g.shape[0] // shards, width) for g in grads]
    return pl.pallas_call(
        functools.partial(scatter_kernel, slab_bits, lat_bits),
        out_shape=[jax.ShapeDtypeStruct((g.shape[0] // shards, width), jnp.float32) for g in grads],
        in_specs=[pl.BlockSpec(memory_space=pltpu.VMEM)] * 4,
        out_specs=[pl.BlockSpec(memory_space=pltpu.VMEM)] * 4,
        scratch_shapes=[pltpu.VMEM(s, jnp.bfloat16) for row in shapes for s in row]
        + [pltpu.VMEM(s, jnp.bfloat16) for row in shapes for s in row[:-1]]
        + [pltpu.SemaphoreType.DMA((4, steps)), pltpu.SemaphoreType.DMA((4, steps))],
        compiler_params=pltpu.CompilerParams(
            collective_id=1, has_side_effects=True, vmem_limit_bytes=40 * 1024 * 1024
        ),
        name="scatter_grads",
    )(
        *(
            g.astype(jnp.bfloat16).reshape(
                (2,) * slab_bits + (lat_count, g.shape[0] // shards, width)
            )
            for g in grads
        )
    )


def from_behind(value, axis, steps):
    count = lax.axis_size(axis)
    first, last = (max(0, -steps), min(count, count - steps))
    return lax.ppermute(value, axis, [(source, source + steps) for source in range(first, last)])


def layer_norm(values, gain_vector):
    average = jnp.mean(values, axis=-1, keepdims=True)
    centred = values - average
    variance = jnp.mean(centred * centred, axis=-1, keepdims=True)
    inverse = lax.rsqrt(variance + EPSILON)
    normed = centred * inverse
    return (normed * gain_vector, normed, inverse)


def norm_back(upstream, normed, inverse, gain_vector):
    scaled = upstream * gain_vector
    return inverse * (
        scaled
        - jnp.mean(scaled, axis=-1, keepdims=True)
        - normed * jnp.mean(scaled * normed, axis=-1, keepdims=True)
    )


def contract_rows(left, right):
    return lax.dot_general(
        left, right, (((0,), (0,)), ((), ())), preferred_element_type=jnp.float32
    )


def times_transpose(left, weight):
    return lax.dot_general(
        left, weight, (((1,), (1,)), ((), ())), preferred_element_type=jnp.float32
    )


def pick_blocks(source_table, blocks):
    width = source_table.shape[1]
    return jnp.take(source_table.reshape(-1, BLK, width), blocks, axis=0).reshape(-1, width)


def add_blocks(source_table, blocks, values):
    width = source_table.shape[1]
    shaped = source_table.reshape(-1, BLK, width).at[blocks].add(values.reshape(-1, BLK, width))
    return shaped.reshape(-1, width)


def per_device(
    nodes,
    edges,
    edge_tiles,
    edge_offsets,
    tile_counts,
    halo_blocks,
    w_edge_in,
    w_edge_out,
    w_node_in,
    w_node_out,
    edge_gain,
    node_gain,
    node_cotangent,
    edge_cotangent,
):
    lat_size = lax.axis_size("lat")
    lat_index = lax.axis_index("lat")
    slab_rows = nodes.shape[0]
    own_rows = slab_rows // lat_size
    halo_rows = HB * BLK
    edge_in, edge_out, node_in, node_out = gather_weights(
        (w_edge_in, w_edge_out, w_node_in, w_node_out), lax.axis_size("slab"), lat_size
    )
    up_list = halo_blocks[0, 0]
    down_list = halo_blocks[0, 1]
    from_lower = from_behind(pick_blocks(nodes, up_list), "slab", 1)
    from_upper = from_behind(pick_blocks(nodes, down_list), "slab", -1)
    extended = lax.all_gather(
        jnp.concatenate([from_lower, nodes, from_upper], axis=0), "lat", axis=1, tiled=True
    )
    slab_full = extended[halo_rows : halo_rows + slab_rows]
    tile_slots = edge_tiles.shape[1]
    tile_of = jnp.arange(edges.shape[0], dtype=jnp.int32) // BLK
    dst_row = edge_tiles[0][tile_of] * BLK + edge_offsets[0]
    src_row = edge_tiles[1][tile_of] * BLK + edge_offsets[1]
    live_mask = (lat_index * tile_slots + tile_of < tile_counts[0]).astype(jnp.float32)[:, None]
    joined = jnp.concatenate([edges, extended[src_row], slab_full[dst_row]], axis=1)
    edge_first = jax.nn.relu(jnp.dot(joined, edge_in, preferred_element_type=jnp.float32)).astype(
        jnp.bfloat16
    )
    edge_second = jnp.dot(edge_first, edge_out, preferred_element_type=jnp.float32)
    edge_update, edge_normed, edge_inverse = layer_norm(edge_second, edge_gain)
    message = edge_update * live_mask
    new_edges = (edges.astype(jnp.float32) + message).astype(jnp.bfloat16)
    partial_sums = jnp.zeros((slab_rows, L), jnp.float32).at[dst_row].add(message)
    aggregated = lax.psum_scatter(partial_sums, "lat", scatter_dimension=0, tiled=True).astype(
        jnp.bfloat16
    )
    row_start = lat_index * own_rows
    own_latents = lax.dynamic_slice_in_dim(slab_full, row_start, own_rows, 0)
    node_joined = jnp.concatenate([own_latents, aggregated], axis=1)
    node_first = jax.nn.relu(
        jnp.dot(node_joined, node_in, preferred_element_type=jnp.float32)
    ).astype(jnp.bfloat16)
    node_second = jnp.dot(node_first, node_out, preferred_element_type=jnp.float32)
    node_update, node_normed, node_inverse = layer_norm(node_second, node_gain)
    new_rows = (own_latents.astype(jnp.float32) + node_update).astype(jnp.bfloat16)
    new_nodes = lax.all_to_all(new_rows, "lat", split_axis=1, concat_axis=0, tiled=True)
    node_upstream = lax.all_to_all(
        node_cotangent, "lat", split_axis=0, concat_axis=1, tiled=True
    ).astype(jnp.float32)
    d_node_second = norm_back(node_upstream, node_normed, node_inverse, node_gain).astype(
        jnp.bfloat16
    )
    g_node_out = contract_rows(node_first, d_node_second)
    d_node_first = (times_transpose(d_node_second, node_out) * (node_first > 0)).astype(
        jnp.bfloat16
    )
    g_node_in = contract_rows(node_joined, d_node_first)
    d_node_joined = times_transpose(d_node_first, node_in)
    d_direct = d_node_joined[:, :L]
    d_aggregated = d_node_joined[:, L:].astype(jnp.bfloat16)
    d_agg_slab = lax.all_gather(d_aggregated, "lat", axis=0, tiled=True)
    edge_upstream = edge_cotangent.astype(jnp.float32)
    d_message = (edge_upstream + d_agg_slab[dst_row].astype(jnp.float32)) * live_mask
    d_edge_second = norm_back(d_message, edge_normed, edge_inverse, edge_gain).astype(jnp.bfloat16)
    g_edge_out = contract_rows(edge_first, d_edge_second)
    d_edge_first = (times_transpose(d_edge_second, edge_out) * (edge_first > 0)).astype(
        jnp.bfloat16
    )
    g_edge_in = contract_rows(joined, d_edge_first)
    d_joined = times_transpose(d_edge_first, edge_in)
    grad_edges = (edge_upstream + d_joined[:, :L]).astype(jnp.bfloat16)
    d_extended = jnp.zeros((extended.shape[0], L), jnp.float32)
    d_extended = d_extended.at[src_row].add(d_joined[:, L : 2 * L])
    d_extended = d_extended.at[halo_rows + dst_row].add(d_joined[:, 2 * L :])
    own_start = halo_rows + row_start
    own_grads = lax.dynamic_slice_in_dim(d_extended, own_start, own_rows, 0) + d_direct
    d_extended = lax.dynamic_update_slice_in_dim(d_extended, own_grads, own_start, 0)
    d_narrow = lax.psum_scatter(
        d_extended.astype(jnp.bfloat16), "lat", scatter_dimension=1, tiled=True
    ).astype(jnp.float32)
    from_above = from_behind(d_narrow[:halo_rows].astype(jnp.bfloat16), "slab", -1).astype(
        jnp.float32
    )
    from_below = from_behind(
        d_narrow[halo_rows + slab_rows :].astype(jnp.bfloat16), "slab", 1
    ).astype(jnp.float32)
    grad_slab = add_blocks(
        add_blocks(d_narrow[halo_rows : halo_rows + slab_rows], up_list, from_above),
        down_list,
        from_below,
    )
    grad_nodes = grad_slab.astype(jnp.bfloat16)
    reduced_grads = scatter_grads(
        (g_edge_in, g_edge_out, g_node_in, g_node_out), lax.axis_size("slab"), lat_size
    )
    return (
        new_nodes,
        new_edges,
        grad_nodes,
        grad_edges,
        reduced_grads[0],
        reduced_grads[1],
        reduced_grads[2],
        reduced_grads[3],
    )


def solution(mesh):
    placed = (
        P("slab", "lat"),
        P(("slab", "lat"), None),
        P(None, ("slab", "lat")),
        P(None, ("slab", "lat")),
        P("slab"),
        P("slab", None, None),
        P(("slab", "lat"), None),
        P(("slab", "lat"), None),
        P(("slab", "lat"), None),
        P(("slab", "lat"), None),
        P(),
        P(),
        P("slab", "lat"),
        P(("slab", "lat"), None),
    )
    return jax.shard_map(
        per_device,
        mesh=mesh,
        in_specs=placed,
        out_specs=(
            P("slab", "lat"),
            P(("slab", "lat"), None),
            P("slab", "lat"),
            P(("slab", "lat"), None),
            P(("slab", "lat"), None),
            P(("slab", "lat"), None),
            P(("slab", "lat"), None),
            P(("slab", "lat"), None),
        ),
        check_vma=False,
    )
```

```python
import functools
import itertools
import types

import jax
import jax.numpy as jnp
from jax import lax
from jax.experimental import pallas as pl
from jax.experimental.pallas import tpu as pltpu
from jax.sharding import PartitionSpec as P

L = 512
BLK = 128
HB = 2


EPSILON = 1e-05

MESH = pl.DeviceIdType.MESH
GROUP_OF = (0, 1, 0, 1)


def pieces_of(rows, group):
    head = rows * 2 // 3 // 16 * 16
    if rows % 16 or not 0 < head < rows or group:
        return [(0, rows, group)]
    return [(0, head, 0), (head, rows - head, 1)] if rows >= 48 else [(0, rows, group)]


def bits_of(count):
    return count.bit_length() - 1


def bit_at(index, b):
    return lax.rem(lax.div(index, 1 << b), 2)


def partner(axis, b):
    index = lax.axis_index(axis)
    return {axis: index + (1 - 2 * bit_at(index, b)) * (1 << b)}


def layer_norm(values, gain_vector):
    average = jnp.mean(values, axis=-1, keepdims=True)
    centred = values - average
    variance = jnp.mean(centred * centred, axis=-1, keepdims=True)
    inverse = lax.rsqrt(variance + EPSILON)
    normed = centred * inverse
    return (normed * gain_vector, normed, inverse)


def norm_back(upstream, normed, inverse, gain_vector):
    scaled = upstream * gain_vector
    return inverse * (
        scaled
        - jnp.mean(scaled, axis=-1, keepdims=True)
        - normed * jnp.mean(scaled * normed, axis=-1, keepdims=True)
    )


def contract_rows(left, right):
    return lax.dot_general(
        left, right, (((0,), (0,)), ((), ())), preferred_element_type=jnp.float32
    )


def times_transpose(left, weight):
    return lax.dot_general(
        left, weight, (((1,), (1,)), ((), ())), preferred_element_type=jnp.float32
    )


def slab_order(slab_bits, group):
    rest = list(range(1, slab_bits))
    return [0] + (rest if group == 0 else rest[::-1])


def dot(left, right):
    return jnp.dot(left, right, preferred_element_type=jnp.float32)


def sum_shapes(slab_bits, lat_count, rows, width):
    shapes = [(2,) * (slab_bits - 1 - k) + (lat_count, rows, width) for k in range(slab_bits)]
    while lat_count > 1:
        lat_count //= 2
        shapes.append((lat_count, rows, width))
    return shapes


def spots_of(slab_bits, lat_count):
    return list(itertools.product(*([range(2)] * slab_bits + [range(lat_count)])))


def layer_kernel(slab_bits, lat_bits, names, *refs):
    r = types.SimpleNamespace()
    for name, ref in zip(names, refs):
        if isinstance(name, str):
            setattr(r, name, ref)
        else:
            vars(r).setdefault(name[0], []).append(ref)
    r.got = [r.got[n : n + slab_bits + lat_bits] for n in range(0, len(r.got), slab_bits + lat_bits)]
    held_steps = slab_bits + lat_bits - 1
    r.held = [r.held[n : n + held_steps] for n in range(0, len(r.held), held_steps)]
    slab_count, lat_count = 1 << slab_bits, 1 << lat_bits
    steps = slab_bits + lat_bits
    slab, lat = lax.axis_index("slab"), lax.axis_index("lat")
    slab_at = [bit_at(slab, b) for b in range(slab_bits)]
    send_sem, recv_sem = r.send_sem, r.recv_sem
    slab_rows, width = r.nodes.shape
    own_rows = slab_rows // lat_count
    halo_rows = HB * BLK
    all_rows = slab_rows + 2 * halo_rows
    edge_rows = r.edges.shape[0]
    tiles = edge_rows // BLK
    bf16, f32 = jnp.bfloat16, jnp.float32
    has_lower, has_upper = slab > 0, slab < slab_count - 1
    lower, upper = {"slab": slab - 1}, {"slab": slab + 1}
    sems = itertools.count()
    sent = []

    def remote(source, target, to):
        k = next(sems)
        return pltpu.make_async_remote_copy(
            src_ref=source,
            dst_ref=target,
            send_sem=send_sem.at[k],
            recv_sem=recv_sem.at[k],
            device_id=to,
            device_id_type=MESH,
        )

    def begin(copy):
        copy.start()
        sent.append(copy)
        return copy

    def peer(k):
        return lax.rem(lat + k, lat_count)

    barrier = pltpu.get_barrier_semaphore()
    for b in range(slab_bits):
        pl.semaphore_signal(barrier, inc=1, device_id=partner("slab", b), device_id_type=MESH)
    for k in range(1, lat_count):
        pl.semaphore_signal(barrier, inc=1, device_id={"lat": peer(k)}, device_id_type=MESH)

    @pl.when(has_lower)
    def _():
        pl.semaphore_signal(barrier, inc=1, device_id=lower, device_id_type=MESH)

    @pl.when(has_upper)
    def _():
        pl.semaphore_signal(barrier, inc=1, device_id=upper, device_id_type=MESH)

    pl.semaphore_wait(
        barrier, slab_bits + lat_count - 1 + has_lower.astype(jnp.int32) + has_upper.astype(jnp.int32)
    )

    shards = [r.w0, r.w1, r.w2, r.w3]
    pieces = [(i, *p) for i in range(4) for p in pieces_of(shards[i].shape[0], GROUP_OF[i])]
    count = len(pieces)
    fulls = r.full
    for (i, start, rows, _), full in zip(pieces, fulls):
        full[tuple(slab_at[::-1]) + (lat,)] = shards[i][start : start + rows, :]

    def gather_start(p, step):
        full = fulls[p]
        order = slab_order(slab_bits, pieces[p][3])[::-1]
        if step < lat_bits:
            size = 1 << step
            spot = tuple(slab_at[::-1]) + (pl.ds(lax.div(lat, size) * size, size),)
            to = partner("lat", step)
        else:
            done = order[: step - lat_bits]
            spot = tuple(
                slice(None) if b in done else slab_at[b] for b in reversed(range(slab_bits))
            )
            to = partner("slab", order[step - lat_bits])
        gathers[p].append(begin(remote(full.at[spot], full.at[spot], to)))

    gathers = [[] for _ in pieces]
    edge_pieces = [p for p in range(count) if pieces[p][0] < 2]
    node_pieces = [p for p in range(count) if pieces[p][0] >= 2]

    def gather_step(which, step):
        for p in which:
            if step >= 0:
                gathers[p][step].wait_recv()
            if step + 1 < steps:
                gather_start(p, step + 1)

    gather_step(edge_pieces, -1)

    def whole(i):
        mine = [fulls[p] for p in range(count) if pieces[p][0] == i]
        rows, cols = shards[i].shape
        total = rows << steps
        if rows % 16 == 0:
            blocks = [full[...].reshape(-1, full.shape[-2], cols) for full in mine]
            return jnp.concatenate(blocks, axis=1).reshape(total, cols)
        full, wide = mine[0], r.wide
        for n, spot in enumerate(spots_of(slab_bits, lat_count)):
            wide[n * rows : (n + 1) * rows, :] = full[spot].astype(f32)
        return wide[0:total, :].astype(bf16)

    own, low, up, cot = r.own, r.low, r.up, r.cot
    own[lat] = r.nodes[...]
    own_copies, cot_copies = [], []
    for k in range(1, lat_count):
        own_copies.append(begin(remote(r.nodes, own.at[lat], {"lat": peer(k)})))

    def places(which, count):
        pieces = [
            r.edge_offsets[which : which + 1, t * BLK : (t + 1) * BLK]
            + r.edge_tiles[which, t] * BLK
            for t in range(tiles)
        ]
        row = jnp.concatenate(pieces, axis=1)
        cells = lax.broadcasted_iota(jnp.int32, (count, edge_rows), 0)
        return jnp.where(cells == row, 1.0, 0.0).astype(bf16)

    r.recv_hot[...] = places(0, slab_rows)
    r.send_hot[...] = places(1, all_rows)
    chunk = 2 * BLK
    parts = edge_rows // chunk

    def rows_of(n):
        return pl.ds(pl.multiple_of(n * chunk, chunk), chunk)

    def live_of(n):
        tile = lat * tiles + (
            n * chunk + lax.broadcasted_iota(jnp.int32, (chunk, 1), 0)
        ) // BLK
        return jnp.where(tile < r.tile_counts[0], 1.0, 0.0).astype(f32)

    gather_step(edge_pieces, 0)
    for copy in own_copies:
        copy.wait_recv()
    for side, staged in ((0, r.to_upper), (1, r.to_lower)):
        for j in range(HB):
            picked = jnp.zeros((lat_count, BLK, width), f32)
            for block in range(slab_rows // BLK):
                hit = (r.halo_blocks[0, side, j] == block).astype(f32)
                picked = picked + hit * own[:, block * BLK : (block + 1) * BLK, :].astype(f32)
            staged[:, j * BLK : (j + 1) * BLK, :] = picked.astype(bf16)

    def halo_exchange(to_upper, to_lower, low_place, up_place):
        upward = remote(to_upper, low_place, upper)
        downward = remote(to_lower, up_place, lower)

        @pl.when(has_upper)
        def _():
            upward.start()

        @pl.when(has_lower)
        def _():
            downward.start()

        def arrive():
            @pl.when(has_lower)
            def _():
                upward.wait_recv()

            @pl.when(jnp.logical_not(has_lower))
            def _():
                low_place[...] = jnp.zeros(low_place.shape, low_place.dtype)

            @pl.when(has_upper)
            def _():
                downward.wait_recv()

            @pl.when(jnp.logical_not(has_upper))
            def _():
                up_place[...] = jnp.zeros(up_place.shape, up_place.dtype)

        def leave():
            @pl.when(has_upper)
            def _():
                upward.wait_send()

            @pl.when(has_lower)
            def _():
                downward.wait_send()

        return arrive, leave

    arrive, leave_latents = halo_exchange(r.to_upper, r.to_lower, low, up)
    for step in range(1, steps - 1):
        gather_step(edge_pieces, step)
        gather_step(node_pieces, step - 2)
    arrive()
    ext = r.ext
    for t in range(lat_count):
        cols = slice(t * width, (t + 1) * width)
        ext[0:halo_rows, cols] = low[t]
        ext[halo_rows : halo_rows + slab_rows, cols] = own[t]
        ext[halo_rows + slab_rows :, cols] = up[t]
    joined = r.joined
    joined[0] = r.edges[...]
    joined[1] = contract_rows(r.send_hot[...], ext[...]).astype(bf16)
    joined[2] = contract_rows(
        r.recv_hot[...], ext[halo_rows : halo_rows + slab_rows, :]
    ).astype(bf16)
    gather_step(edge_pieces, steps - 1)
    gather_step(node_pieces, steps - 3)
    edge_in, edge_out, node_in, node_out = r.mat0, r.mat1, r.mat2, r.mat3
    edge_in[...], edge_out[...] = whole(0), whole(1)
    edge_gain, node_gain = r.edge_gain[...], r.node_gain[...]

    def edge_forward(n, carry):
        rows = rows_of(n)
        first = dot(joined[0, rows, :], edge_in[0:L, :])
        first += dot(joined[1, rows, :], edge_in[L : 2 * L, :])
        first += dot(joined[2, rows, :], edge_in[2 * L :, :])
        first = jnp.maximum(first, 0.0).astype(bf16)
        r.first[rows, :] = first
        update, normed, inverse = layer_norm(dot(first, edge_out[...]), edge_gain)
        r.normed[rows, :] = normed
        r.inverse[rows, :] = inverse
        message = update * live_of(n)
        r.new_edges[rows, :] = (r.edges[rows, :].astype(f32) + message).astype(bf16)
        top = message.astype(bf16)
        r.top[rows, :] = top
        r.rest[rows, :] = (message - top.astype(f32)).astype(bf16)
        return carry

    half = parts // 2
    lax.fori_loop(0, half, edge_forward, 0)
    gather_step(node_pieces, steps - 2)
    lax.fori_loop(half, parts, edge_forward, 0)
    sums = dot(r.recv_hot[...], r.top[...]) + dot(r.recv_hot[...], r.rest[...])
    r.sums[...] = sums.reshape(lat_count, own_rows, L)
    sum_copies = [
        begin(remote(r.sums.at[peer(k)], r.sums_got.at[k - 1], {"lat": peer(k)}))
        for k in range(1, lat_count)
    ]
    for k in range(1, lat_count):
        rows = pl.ds(pl.multiple_of(peer(k) * own_rows, own_rows), own_rows)
        cot_copies.append(
            begin(remote(r.node_cotangent.at[rows], cot.at[lat], {"lat": peer(k)}))
        )
    cot[lat] = r.node_cotangent[pl.ds(pl.multiple_of(lat * own_rows, own_rows), own_rows), :]
    gather_step(node_pieces, steps - 1)
    node_in[...], node_out[...] = whole(2), whole(3)
    own_latents = ext[pl.ds(pl.multiple_of(halo_rows + lat * own_rows, own_rows), own_rows), :]
    for copy in cot_copies:
        copy.wait_recv()
    upstream = jnp.concatenate([cot[t] for t in range(lat_count)], axis=1).astype(f32)
    node_pre = dot(own_latents, node_in[0:L, :])
    total = r.sums[lat]
    for k, copy in enumerate(sum_copies):
        copy.wait_recv()
        total = total + r.sums_got[k]
    aggregated = total.astype(bf16)

    node_first = jnp.maximum(node_pre + dot(aggregated, node_in[L:, :]), 0.0).astype(bf16)
    update, normed, inverse = layer_norm(dot(node_first, node_out[...]), node_gain)
    new_rows = (own_latents.astype(f32) + update).astype(bf16)
    d_second = norm_back(upstream, normed, inverse, node_gain).astype(bf16)
    d_first = (times_transpose(d_second, node_out[...]) * (node_first > 0).astype(f32)).astype(bf16)
    d_agg = r.d_agg
    d_agg[lat] = times_transpose(d_first, node_in[L:, :]).astype(bf16)
    agg_copies = [
        begin(remote(d_agg.at[lat], d_agg.at[lat], {"lat": peer(k)})) for k in range(1, lat_count)
    ]
    for t in range(lat_count):
        r.rows_out[t] = new_rows[:, t * width : (t + 1) * width]
    r.new_nodes[lat] = r.rows_out[lat]
    out_copies = [
        begin(remote(r.rows_out.at[peer(k)], r.new_nodes.at[lat], {"lat": peer(k)}))
        for k in range(1, lat_count)
    ]

    sum_refs, got, held = r.grad, r.got, r.held
    grad_outs = [r.grad_out0, r.grad_out1, r.grad_out2, r.grad_out3]
    scatters = [[] for _ in pieces]

    def scatter_plan(i, step):
        if step < slab_bits:
            order = slab_order(slab_bits, pieces[i][3])
            b = order[step]
            left = sorted(set(range(slab_bits)) - set(order[:step]), reverse=True)
            lead = (slice(None),) * left.index(b)
            return lead + (slab_at[b],), lead + (1 - slab_at[b],), partner("slab", b)
        b = lat_bits - 1 - (step - slab_bits)
        size = 1 << b
        mine = bit_at(lat, b)
        return (pl.ds(mine * size, size),), (pl.ds((1 - mine) * size, size),), partner("lat", b)

    def scatter_source(i, step):
        return sum_refs[i] if step == 0 else held[i][step - 1]

    def scatter_start(i, step):
        _, theirs, to = scatter_plan(i, step)
        scatters[i].append(
            begin(remote(scatter_source(i, step).at[theirs], got[i][step], to))
        )

    def scatter_step(i, step):
        scatters[i][step].wait_recv()
        mine, _, _ = scatter_plan(i, step)
        total = scatter_source(i, step)[mine].astype(f32) + got[i][step][...].astype(f32)
        if step + 1 < steps:
            held[i][step][...] = total.astype(bf16)
            scatter_start(i, step + 1)
        else:
            k, start, rows, _ = pieces[i]
            grad_outs[k][start : start + rows, :] = total.reshape(rows, total.shape[-1])

    def put_grad(i, values):
        rows = shards[i].shape[0]
        mine = [p for p in range(count) if pieces[p][0] == i]
        if rows % 16 == 0:
            cut = values.astype(bf16).reshape(-1, rows, values.shape[1])
            for p in mine:
                _, start, some, _ = pieces[p]
                sum_refs[p][...] = cut[:, start : start + some, :].reshape(sum_refs[p].shape)
        else:
            wide = r.wide
            wide[0 : values.shape[0], :] = values
            for n, spot in enumerate(spots_of(slab_bits, lat_count)):
                sum_refs[mine[0]][spot] = wide[n * rows : (n + 1) * rows, :].astype(bf16)
        for p in mine:
            scatter_start(p, 0)

    put_grad(3, contract_rows(node_first, d_second))
    put_grad(
        2, contract_rows(jnp.concatenate([own_latents, aggregated], axis=1), d_first)
    )
    d_direct = times_transpose(d_first, node_in[0:L, :])
    for p in node_pieces:
        scatter_step(p, 0)

    for copy in agg_copies:
        copy.wait_recv()
    r.d_edge[...] = contract_rows(
        r.recv_hot[...], d_agg[...].reshape(slab_rows, L)
    ).astype(bf16)

    def edge_second(n, carry):
        rows = rows_of(n)
        d_message = (
            r.edge_cotangent[rows, :].astype(f32) + r.d_edge[rows, :].astype(f32)
        ) * live_of(n)
        d_second = norm_back(d_message, r.normed[rows, :], r.inverse[rows, :], edge_gain)
        r.top[rows, :] = d_second.astype(bf16)
        return carry

    lax.fori_loop(0, parts, edge_second, 0)
    put_grad(1, contract_rows(r.first[...], r.top[...]))
    for p in node_pieces:
        scatter_step(p, 1)

    def edge_first(n, carry):
        rows = rows_of(n)
        d_first = times_transpose(r.top[rows, :], edge_out[...])
        r.rest[rows, :] = (d_first * (r.first[rows, :] > 0).astype(f32)).astype(bf16)
        return carry

    lax.fori_loop(0, parts, edge_first, 0)
    def edge_joined(n, carry):
        rows = rows_of(n)
        d_first = r.rest[rows, :]
        direct = times_transpose(d_first, edge_in[0:L, :])
        r.grad_edges[rows, :] = (
            r.edge_cotangent[rows, :].astype(f32) + direct
        ).astype(bf16)
        r.far[rows, :] = times_transpose(d_first, edge_in[L : 2 * L, :]).astype(bf16)
        r.d_edge[rows, :] = times_transpose(d_first, edge_in[2 * L :, :]).astype(bf16)
        return carry

    lax.fori_loop(0, parts, edge_joined, 0)
    d_ext = r.d_ext
    d_ext[...] = dot(r.send_hot[...], r.far[...])
    d_ext[halo_rows : halo_rows + slab_rows, :] += dot(r.recv_hot[...], r.d_edge[...])
    mine = pl.ds(pl.multiple_of(halo_rows + lat * own_rows, own_rows), own_rows)
    d_ext[mine, :] += d_direct
    r.back_low[...] = d_ext[0:halo_rows, :].astype(bf16)
    r.back_up[...] = d_ext[halo_rows + slab_rows :, :].astype(bf16)
    arrive, leave_grads = halo_exchange(
        r.back_up, r.back_low, r.from_below, r.from_above
    )
    put_grad(
        0,
        jnp.concatenate([contract_rows(joined[k], r.rest[...]) for k in range(3)], axis=0),
    )
    arrive()
    for block in range(slab_rows // BLK):
        rows = slice(halo_rows + block * BLK, halo_rows + (block + 1) * BLK)
        total = d_ext[rows, :]
        for side, place in ((0, r.from_above), (1, r.from_below)):
            for j in range(HB):
                hit = (r.halo_blocks[0, side, j] == block).astype(f32)
                total = total + hit * place[j * BLK : (j + 1) * BLK, :].astype(f32)
        total = total.astype(bf16)
        for t in range(lat_count):
            r.d_cut[t, block * BLK : (block + 1) * BLK, :] = total[
                :, t * width : (t + 1) * width
            ]
    cut_copies = [
        begin(remote(r.d_cut.at[peer(k)], r.d_got.at[k - 1], {"lat": peer(k)}))
        for k in range(1, lat_count)
    ]
    for step in range(steps):
        for p in node_pieces:
            if step + 2 < steps:
                scatter_step(p, step + 2)
        for p in edge_pieces[::-1]:
            scatter_step(p, step)
    narrow = r.d_cut[lat].astype(f32)
    for k, copy in enumerate(cut_copies):
        copy.wait_recv()
        narrow = narrow + r.d_got[k].astype(f32)
    r.grad_nodes[...] = narrow.astype(bf16)
    for copy in out_copies:
        copy.wait_recv()
    for copy in sent:
        copy.wait_send()
    leave_latents()
    leave_grads()


def per_device(
    nodes,
    edges,
    edge_tiles,
    edge_offsets,
    tile_counts,
    halo_blocks,
    w_edge_in,
    w_edge_out,
    w_node_in,
    w_node_out,
    edge_gain,
    node_gain,
    node_cotangent,
    edge_cotangent,
):
    slab_count, lat_count = lax.axis_size("slab"), lax.axis_size("lat")
    slab_bits, lat_bits = bits_of(slab_count), bits_of(lat_count)
    steps = slab_bits + lat_bits
    slab_rows, width = nodes.shape
    own_rows = slab_rows // lat_count
    halo_rows = HB * BLK
    all_rows = slab_rows + 2 * halo_rows
    edge_rows = edges.shape[0]
    bf16, f32 = jnp.bfloat16, jnp.float32
    weights = (w_edge_in, w_edge_out, w_node_in, w_node_out)
    whole_rows = [w.shape[0] * slab_count * lat_count for w in weights]
    vmem, smem = pl.BlockSpec(memory_space=pltpu.VMEM), pl.BlockSpec(memory_space=pltpu.SMEM)
    inputs = dict(
        nodes=nodes,
        edges=edges,
        edge_tiles=edge_tiles,
        edge_offsets=edge_offsets,
        tile_counts=tile_counts,
        halo_blocks=halo_blocks,
        w0=w_edge_in,
        w1=w_edge_out,
        w2=w_node_in,
        w3=w_node_out,
        edge_gain=edge_gain.reshape(1, -1),
        node_gain=node_gain.reshape(1, -1),
        node_cotangent=node_cotangent,
        edge_cotangent=edge_cotangent,
    )
    outputs = dict(
        new_nodes=((lat_count, own_rows, width), bf16),
        new_edges=(edges.shape, bf16),
        grad_nodes=(nodes.shape, bf16),
        grad_edges=(edges.shape, bf16),
        grad_out0=(w_edge_in.shape, f32),
        grad_out1=(w_edge_out.shape, f32),
        grad_out2=(w_node_in.shape, f32),
        grad_out3=(w_node_out.shape, f32),
    )
    scratch = dict(
        own=((lat_count, slab_rows, width), bf16),
        low=((lat_count, halo_rows, width), bf16),
        up=((lat_count, halo_rows, width), bf16),
        to_upper=((lat_count, halo_rows, width), bf16),
        to_lower=((lat_count, halo_rows, width), bf16),
        cot=((lat_count, own_rows, width), bf16),
        recv_hot=((slab_rows, edge_rows), bf16),
        send_hot=((all_rows, edge_rows), bf16),
        ext=((all_rows, L), bf16),
        joined=((3, edge_rows, L), bf16),
        first=((edge_rows, L), bf16),
        normed=((edge_rows, L), f32),
        inverse=((edge_rows, 1), f32),
        top=((edge_rows, L), bf16),
        rest=((edge_rows, L), bf16),
        sums=((lat_count, own_rows, L), f32),
        sums_got=((lat_count - 1, own_rows, L), f32),
        d_agg=((lat_count, own_rows, L), bf16),
        rows_out=((lat_count, own_rows, width), bf16),
        d_edge=((edge_rows, L), bf16),
        d_ext=((all_rows, L), f32),
        d_cut=((lat_count, slab_rows, width), bf16),
        d_got=((lat_count - 1, slab_rows, width), bf16),
        back_low=((halo_rows, L), bf16),
        back_up=((halo_rows, L), bf16),
        from_below=((halo_rows, L), bf16),
        from_above=((halo_rows, L), bf16),
        far=((edge_rows, L), bf16),
        mat0=((whole_rows[0], L), bf16),
        mat1=((whole_rows[1], L), bf16),
        mat2=((whole_rows[2], L), bf16),
        mat3=((whole_rows[3], L), bf16),
        wide=((max(whole_rows), L), f32),
    )
    names, shapes = list(scratch), list(scratch.values())
    for i in range(4):
        for _, rows, _ in pieces_of(weights[i].shape[0], GROUP_OF[i]):
            cut = (2,) * slab_bits + (lat_count, rows, L)
            names += [("full",), ("grad",)]
            shapes += [(cut, bf16)] * 2
            for k, shape in enumerate(sum_shapes(slab_bits, lat_count, rows, L)):
                names.append(("got",))
                shapes.append((shape, bf16))
                if k + 1 < steps:
                    names.append(("held",))
                    shapes.append((shape, bf16))
    count = names.count(("full",))
    copies = 2 * count * steps + 6 * (lat_count - 1) + 4
    results = pl.pallas_call(
        functools.partial(
            layer_kernel,
            slab_bits,
            lat_bits,
            [*inputs, *outputs, *names, "send_sem", "recv_sem"],
        ),
        out_shape=[jax.ShapeDtypeStruct(*o) for o in outputs.values()],
        in_specs=[smem if n in (2, 4, 5) else vmem for n in range(len(inputs))],
        out_specs=[vmem] * len(outputs),
        scratch_shapes=[pltpu.VMEM(*s) for s in shapes]
        + [pltpu.SemaphoreType.DMA((copies,)), pltpu.SemaphoreType.DMA((copies,))],
        compiler_params=pltpu.CompilerParams(
            collective_id=0, has_side_effects=True, vmem_limit_bytes=56 * 1024 * 1024
        ),
        name="mesh_layer",
    )(*inputs.values())
    return (results[0].reshape(nodes.shape), *results[1:])


def solution(mesh):
    placed = (
        P("slab", "lat"),
        P(("slab", "lat"), None),
        P(None, ("slab", "lat")),
        P(None, ("slab", "lat")),
        P("slab"),
        P("slab", None, None),
        P(("slab", "lat"), None),
        P(("slab", "lat"), None),
        P(("slab", "lat"), None),
        P(("slab", "lat"), None),
        P(),
        P(),
        P("slab", "lat"),
        P(("slab", "lat"), None),
    )
    return jax.shard_map(
        per_device,
        mesh=mesh,
        in_specs=placed,
        out_specs=(
            P("slab", "lat"),
            P(("slab", "lat"), None),
            P("slab", "lat"),
            P(("slab", "lat"), None),
            P(("slab", "lat"), None),
            P(("slab", "lat"), None),
            P(("slab", "lat"), None),
            P(("slab", "lat"), None),
        ),
        check_vma=False,
    )
```

```python
import functools
import itertools
import types

import jax
import jax.numpy as jnp
from jax import lax
from jax.experimental import pallas as pl
from jax.experimental.pallas import tpu as pltpu
from jax.sharding import PartitionSpec as P

L = 512
BLK = 128
HB = 2


EPSILON = 1e-05

MESH = pl.DeviceIdType.MESH
GROUP_OF = (0, 1, 0, 1)


def pieces_of(rows, group):
    head = rows * 2 // 3 // 16 * 16
    if rows % 16 or not 0 < head < rows or group:
        return [(0, rows, group)]
    return [(0, head, 0), (head, rows - head, 1)] if rows >= 48 else [(0, rows, group)]


def bits_of(count):
    return count.bit_length() - 1


def bit_at(index, b):
    return lax.rem(lax.div(index, 1 << b), 2)


def partner(axis, b):
    index = lax.axis_index(axis)
    return {axis: index + (1 - 2 * bit_at(index, b)) * (1 << b)}


def layer_norm(values, gain_vector):
    average = jnp.mean(values, axis=-1, keepdims=True)
    centred = values - average
    variance = jnp.mean(centred * centred, axis=-1, keepdims=True)
    inverse = lax.rsqrt(variance + EPSILON)
    normed = centred * inverse
    return (normed * gain_vector, normed, inverse)


def norm_back(upstream, normed, inverse, gain_vector):
    scaled = upstream * gain_vector
    return inverse * (
        scaled
        - jnp.mean(scaled, axis=-1, keepdims=True)
        - normed * jnp.mean(scaled * normed, axis=-1, keepdims=True)
    )


def contract_rows(left, right):
    return lax.dot_general(
        left, right, (((0,), (0,)), ((), ())), preferred_element_type=jnp.float32
    )


def times_transpose(left, weight):
    return lax.dot_general(
        left, weight, (((1,), (1,)), ((), ())), preferred_element_type=jnp.float32
    )


def slab_order(slab_bits, group):
    rest = list(range(1, slab_bits))
    return [0] + (rest if group == 0 else rest[::-1])


def dot(left, right):
    return jnp.dot(left, right, preferred_element_type=jnp.float32)


def sum_shapes(slab_bits, lat_count, rows, width):
    shapes = [(2,) * (slab_bits - 1 - k) + (lat_count, rows, width) for k in range(slab_bits)]
    while lat_count > 1:
        lat_count //= 2
        shapes.append((lat_count, rows, width))
    return shapes


def spots_of(slab_bits, lat_count):
    return list(itertools.product(*([range(2)] * slab_bits + [range(lat_count)])))


def layer_kernel(slab_bits, lat_bits, names, *refs):
    r = types.SimpleNamespace()
    for name, ref in zip(names, refs):
        if isinstance(name, str):
            setattr(r, name, ref)
        else:
            vars(r).setdefault(name[0], []).append(ref)
    r.got = [r.got[n : n + slab_bits + lat_bits] for n in range(0, len(r.got), slab_bits + lat_bits)]
    held_steps = slab_bits + lat_bits - 1
    r.held = [r.held[n : n + held_steps] for n in range(0, len(r.held), held_steps)]
    slab_count, lat_count = 1 << slab_bits, 1 << lat_bits
    steps = slab_bits + lat_bits
    slab, lat = lax.axis_index("slab"), lax.axis_index("lat")
    slab_at = [bit_at(slab, b) for b in range(slab_bits)]
    send_sem, recv_sem = r.send_sem, r.recv_sem
    slab_rows, width = r.nodes.shape
    own_rows = slab_rows // lat_count
    halo_rows = HB * BLK
    all_rows = slab_rows + 2 * halo_rows
    edge_rows = r.edges.shape[0]
    tiles = edge_rows // BLK
    bf16, f32 = jnp.bfloat16, jnp.float32
    has_lower, has_upper = slab > 0, slab < slab_count - 1
    lower, upper = {"slab": slab - 1}, {"slab": slab + 1}
    sems = itertools.count()
    sent = []

    def remote(source, target, to):
        k = next(sems)
        return pltpu.make_async_remote_copy(
            src_ref=source,
            dst_ref=target,
            send_sem=send_sem.at[k],
            recv_sem=recv_sem.at[k],
            device_id=to,
            device_id_type=MESH,
        )

    def begin(copy):
        copy.start()
        sent.append(copy)
        return copy

    def peer(k):
        return lax.rem(lat + k, lat_count)

    barrier = pltpu.get_barrier_semaphore()
    for b in range(slab_bits):
        pl.semaphore_signal(barrier, inc=1, device_id=partner("slab", b), device_id_type=MESH)
    for k in range(1, lat_count):
        pl.semaphore_signal(barrier, inc=1, device_id={"lat": peer(k)}, device_id_type=MESH)

    @pl.when(has_lower)
    def _():
        pl.semaphore_signal(barrier, inc=1, device_id=lower, device_id_type=MESH)

    @pl.when(has_upper)
    def _():
        pl.semaphore_signal(barrier, inc=1, device_id=upper, device_id_type=MESH)

    pl.semaphore_wait(
        barrier, slab_bits + lat_count - 1 + has_lower.astype(jnp.int32) + has_upper.astype(jnp.int32)
    )

    shards = [r.w0, r.w1, r.w2, r.w3]
    pieces = [(i, *p) for i in range(4) for p in pieces_of(shards[i].shape[0], GROUP_OF[i])]
    count = len(pieces)
    fulls = r.full
    for (i, start, rows, _), full in zip(pieces, fulls):
        full[tuple(slab_at[::-1]) + (lat,)] = shards[i][start : start + rows, :]

    def gather_start(p, step):
        full = fulls[p]
        order = slab_order(slab_bits, pieces[p][3])[::-1]
        if step < lat_bits:
            size = 1 << step
            spot = tuple(slab_at[::-1]) + (pl.ds(lax.div(lat, size) * size, size),)
            to = partner("lat", step)
        else:
            done = order[: step - lat_bits]
            spot = tuple(
                slice(None) if b in done else slab_at[b] for b in reversed(range(slab_bits))
            )
            to = partner("slab", order[step - lat_bits])
        gathers[p].append(begin(remote(full.at[spot], full.at[spot], to)))

    gathers = [[] for _ in pieces]
    edge_pieces = [p for p in range(count) if pieces[p][0] < 2]
    node_pieces = [p for p in range(count) if pieces[p][0] >= 2]

    def gather_step(which, step):
        for p in which:
            if step >= 0:
                gathers[p][step].wait_recv()
            if step + 1 < steps:
                gather_start(p, step + 1)

    gather_step(edge_pieces, -1)

    def whole(i):
        mine = [fulls[p] for p in range(count) if pieces[p][0] == i]
        rows, cols = shards[i].shape
        total = rows << steps
        if rows % 16 == 0:
            blocks = [full[...].reshape(-1, full.shape[-2], cols) for full in mine]
            return jnp.concatenate(blocks, axis=1).reshape(total, cols)
        full, wide = mine[0], r.wide
        for n, spot in enumerate(spots_of(slab_bits, lat_count)):
            wide[n * rows : (n + 1) * rows, :] = full[spot].astype(f32)
        return wide[0:total, :].astype(bf16)

    own, low, up, cot = r.own, r.low, r.up, r.cot
    own[lat] = r.nodes[...]
    own_copies, cot_copies = [], []
    for k in range(1, lat_count):
        own_copies.append(begin(remote(r.nodes, own.at[lat], {"lat": peer(k)})))

    def places(which, count):
        pieces = [
            r.edge_offsets[which : which + 1, t * BLK : (t + 1) * BLK]
            + r.edge_tiles[which, t] * BLK
            for t in range(tiles)
        ]
        row = jnp.concatenate(pieces, axis=1)
        cells = lax.broadcasted_iota(jnp.int32, (count, edge_rows), 0)
        return jnp.where(cells == row, 1.0, 0.0).astype(bf16)

    r.recv_hot[...] = places(0, slab_rows)
    r.send_hot[...] = places(1, all_rows)
    r.recv_turned[...] = r.recv_hot[...].T
    r.send_turned[...] = r.send_hot[...].T
    chunk = 2 * BLK
    parts = edge_rows // chunk

    def rows_of(n):
        return pl.ds(pl.multiple_of(n * chunk, chunk), chunk)

    def live_of(n):
        tile = lat * tiles + (
            n * chunk + lax.broadcasted_iota(jnp.int32, (chunk, 1), 0)
        ) // BLK
        return jnp.where(tile < r.tile_counts[0], 1.0, 0.0).astype(f32)

    gather_step(edge_pieces, 0)
    for copy in own_copies:
        copy.wait_recv()
    for side, staged in ((0, r.to_upper), (1, r.to_lower)):
        for j in range(HB):
            picked = jnp.zeros((lat_count, BLK, width), f32)
            for block in range(slab_rows // BLK):
                hit = (r.halo_blocks[0, side, j] == block).astype(f32)
                picked = picked + hit * own[:, block * BLK : (block + 1) * BLK, :].astype(f32)
            staged[:, j * BLK : (j + 1) * BLK, :] = picked.astype(bf16)

    def halo_exchange(to_upper, to_lower, low_place, up_place):
        upward = remote(to_upper, low_place, upper)
        downward = remote(to_lower, up_place, lower)

        @pl.when(has_upper)
        def _():
            upward.start()

        @pl.when(has_lower)
        def _():
            downward.start()

        def arrive():
            @pl.when(has_lower)
            def _():
                upward.wait_recv()

            @pl.when(jnp.logical_not(has_lower))
            def _():
                low_place[...] = jnp.zeros(low_place.shape, low_place.dtype)

            @pl.when(has_upper)
            def _():
                downward.wait_recv()

            @pl.when(jnp.logical_not(has_upper))
            def _():
                up_place[...] = jnp.zeros(up_place.shape, up_place.dtype)

        def leave():
            @pl.when(has_upper)
            def _():
                upward.wait_send()

            @pl.when(has_lower)
            def _():
                downward.wait_send()

        return arrive, leave

    arrive, leave_latents = halo_exchange(r.to_upper, r.to_lower, low, up)
    for step in range(1, steps - 1):
        gather_step(edge_pieces, step)
        gather_step(node_pieces, step - 2)
    arrive()
    ext = r.ext
    for t in range(lat_count):
        cols = slice(t * width, (t + 1) * width)
        ext[0:halo_rows, cols] = low[t]
        ext[halo_rows : halo_rows + slab_rows, cols] = own[t]
        ext[halo_rows + slab_rows :, cols] = up[t]
    joined = r.joined
    joined[0] = r.edges[...]
    joined[1] = dot(r.send_turned[...], ext[...]).astype(bf16)
    joined[2] = dot(
        r.recv_turned[...], ext[halo_rows : halo_rows + slab_rows, :]
    ).astype(bf16)
    gather_step(edge_pieces, steps - 1)
    gather_step(node_pieces, steps - 3)
    edge_in, edge_out, node_in, node_out = r.mat0, r.mat1, r.mat2, r.mat3
    edge_in[...], edge_out[...] = whole(0), whole(1)
    edge_gain, node_gain = r.edge_gain[...], r.node_gain[...]

    def edge_forward(n, carry):
        rows = rows_of(n)
        first = dot(joined[0, rows, :], edge_in[0:L, :])
        first += dot(joined[1, rows, :], edge_in[L : 2 * L, :])
        first += dot(joined[2, rows, :], edge_in[2 * L :, :])
        first = jnp.maximum(first, 0.0).astype(bf16)
        r.first[rows, :] = first
        update, normed, inverse = layer_norm(dot(first, edge_out[...]), edge_gain)
        r.normed[rows, :] = normed
        r.inverse[rows, :] = inverse
        message = update * live_of(n)
        r.new_edges[rows, :] = (r.edges[rows, :].astype(f32) + message).astype(bf16)
        top = message.astype(bf16)
        r.top[rows, :] = top
        r.rest[rows, :] = (message - top.astype(f32)).astype(bf16)
        return carry

    half = parts // 2
    lax.fori_loop(0, half, edge_forward, 0)
    gather_step(node_pieces, steps - 2)
    lax.fori_loop(half, parts, edge_forward, 0)
    sums = dot(r.recv_hot[...], r.top[...]) + dot(r.recv_hot[...], r.rest[...])
    r.sums[...] = sums.reshape(lat_count, own_rows, L)
    sum_copies = [
        begin(remote(r.sums.at[peer(k)], r.sums_got.at[k - 1], {"lat": peer(k)}))
        for k in range(1, lat_count)
    ]
    for k in range(1, lat_count):
        rows = pl.ds(pl.multiple_of(peer(k) * own_rows, own_rows), own_rows)
        cot_copies.append(
            begin(remote(r.node_cotangent.at[rows], cot.at[lat], {"lat": peer(k)}))
        )
    cot[lat] = r.node_cotangent[pl.ds(pl.multiple_of(lat * own_rows, own_rows), own_rows), :]
    for k in range(3):
        r.joined_turned[k] = joined[k].T
    r.first_turned[...] = r.first[...].T
    gather_step(node_pieces, steps - 1)
    node_in[...], node_out[...] = whole(2), whole(3)
    own_latents = ext[pl.ds(pl.multiple_of(halo_rows + lat * own_rows, own_rows), own_rows), :]
    for copy in cot_copies:
        copy.wait_recv()
    upstream = jnp.concatenate([cot[t] for t in range(lat_count)], axis=1).astype(f32)
    node_pre = dot(own_latents, node_in[0:L, :])
    total = r.sums[lat]
    for k, copy in enumerate(sum_copies):
        copy.wait_recv()
        total = total + r.sums_got[k]
    aggregated = total.astype(bf16)

    node_first = jnp.maximum(node_pre + dot(aggregated, node_in[L:, :]), 0.0).astype(bf16)
    update, normed, inverse = layer_norm(dot(node_first, node_out[...]), node_gain)
    new_rows = (own_latents.astype(f32) + update).astype(bf16)
    d_second = norm_back(upstream, normed, inverse, node_gain).astype(bf16)
    d_first = (times_transpose(d_second, node_out[...]) * (node_first > 0).astype(f32)).astype(bf16)
    d_agg = r.d_agg
    d_agg[lat] = times_transpose(d_first, node_in[L:, :]).astype(bf16)
    agg_copies = [
        begin(remote(d_agg.at[lat], d_agg.at[lat], {"lat": peer(k)})) for k in range(1, lat_count)
    ]
    for t in range(lat_count):
        r.rows_out[t] = new_rows[:, t * width : (t + 1) * width]
    r.new_nodes[lat] = r.rows_out[lat]
    out_copies = [
        begin(remote(r.rows_out.at[peer(k)], r.new_nodes.at[lat], {"lat": peer(k)}))
        for k in range(1, lat_count)
    ]

    sum_refs, got, held = r.grad, r.got, r.held
    grad_outs = [r.grad_out0, r.grad_out1, r.grad_out2, r.grad_out3]
    scatters = [[] for _ in pieces]

    def scatter_plan(i, step):
        if step < slab_bits:
            order = slab_order(slab_bits, pieces[i][3])
            b = order[step]
            left = sorted(set(range(slab_bits)) - set(order[:step]), reverse=True)
            lead = (slice(None),) * left.index(b)
            return lead + (slab_at[b],), lead + (1 - slab_at[b],), partner("slab", b)
        b = lat_bits - 1 - (step - slab_bits)
        size = 1 << b
        mine = bit_at(lat, b)
        return (pl.ds(mine * size, size),), (pl.ds((1 - mine) * size, size),), partner("lat", b)

    def scatter_source(i, step):
        return sum_refs[i] if step == 0 else held[i][step - 1]

    def scatter_start(i, step):
        _, theirs, to = scatter_plan(i, step)
        scatters[i].append(
            begin(remote(scatter_source(i, step).at[theirs], got[i][step], to))
        )

    def scatter_step(i, step):
        scatters[i][step].wait_recv()
        mine, _, _ = scatter_plan(i, step)
        total = scatter_source(i, step)[mine].astype(f32) + got[i][step][...].astype(f32)
        if step + 1 < steps:
            held[i][step][...] = total.astype(bf16)
            scatter_start(i, step + 1)
        else:
            k, start, rows, _ = pieces[i]
            grad_outs[k][start : start + rows, :] = total.reshape(rows, total.shape[-1])

    def put_grad(i, values):
        rows = shards[i].shape[0]
        mine = [p for p in range(count) if pieces[p][0] == i]
        if rows % 16 == 0:
            cut = values.astype(bf16).reshape(-1, rows, values.shape[1])
            for p in mine:
                _, start, some, _ = pieces[p]
                sum_refs[p][...] = cut[:, start : start + some, :].reshape(sum_refs[p].shape)
        else:
            wide = r.wide
            wide[0 : values.shape[0], :] = values
            for n, spot in enumerate(spots_of(slab_bits, lat_count)):
                sum_refs[mine[0]][spot] = wide[n * rows : (n + 1) * rows, :].astype(bf16)
        for p in mine:
            scatter_start(p, 0)

    put_grad(3, contract_rows(node_first, d_second))
    put_grad(
        2, contract_rows(jnp.concatenate([own_latents, aggregated], axis=1), d_first)
    )
    d_direct = times_transpose(d_first, node_in[0:L, :])
    for p in node_pieces:
        scatter_step(p, 0)

    for copy in agg_copies:
        copy.wait_recv()
    r.d_edge[...] = dot(
        r.recv_turned[...], d_agg[...].reshape(slab_rows, L)
    ).astype(bf16)

    def edge_second(n, carry):
        rows = rows_of(n)
        d_message = (
            r.edge_cotangent[rows, :].astype(f32) + r.d_edge[rows, :].astype(f32)
        ) * live_of(n)
        d_second = norm_back(d_message, r.normed[rows, :], r.inverse[rows, :], edge_gain)
        r.top[rows, :] = d_second.astype(bf16)
        return carry

    lax.fori_loop(0, parts, edge_second, 0)
    put_grad(1, dot(r.first_turned[...], r.top[...]))
    for p in node_pieces:
        scatter_step(p, 1)

    def edge_first(n, carry):
        rows = rows_of(n)
        d_first = times_transpose(r.top[rows, :], edge_out[...])
        r.rest[rows, :] = (d_first * (r.first[rows, :] > 0).astype(f32)).astype(bf16)
        return carry

    lax.fori_loop(0, parts, edge_first, 0)
    def edge_joined(n, carry):
        rows = rows_of(n)
        d_first = r.rest[rows, :]
        direct = times_transpose(d_first, edge_in[0:L, :])
        r.grad_edges[rows, :] = (
            r.edge_cotangent[rows, :].astype(f32) + direct
        ).astype(bf16)
        r.first[rows, :] = times_transpose(d_first, edge_in[L : 2 * L, :]).astype(bf16)
        r.d_edge[rows, :] = times_transpose(d_first, edge_in[2 * L :, :]).astype(bf16)
        return carry

    lax.fori_loop(0, parts, edge_joined, 0)
    d_ext = r.d_ext
    d_ext[...] = dot(r.send_hot[...], r.first[...])
    d_ext[halo_rows : halo_rows + slab_rows, :] += dot(r.recv_hot[...], r.d_edge[...])
    mine = pl.ds(pl.multiple_of(halo_rows + lat * own_rows, own_rows), own_rows)
    d_ext[mine, :] += d_direct
    r.back_low[...] = d_ext[0:halo_rows, :].astype(bf16)
    r.back_up[...] = d_ext[halo_rows + slab_rows :, :].astype(bf16)
    arrive, leave_grads = halo_exchange(
        r.back_up, r.back_low, r.from_below, r.from_above
    )
    put_grad(
        0,
        jnp.concatenate([dot(r.joined_turned[k], r.rest[...]) for k in range(3)], axis=0),
    )
    arrive()
    for block in range(slab_rows // BLK):
        rows = slice(halo_rows + block * BLK, halo_rows + (block + 1) * BLK)
        total = d_ext[rows, :]
        for side, place in ((0, r.from_above), (1, r.from_below)):
            for j in range(HB):
                hit = (r.halo_blocks[0, side, j] == block).astype(f32)
                total = total + hit * place[j * BLK : (j + 1) * BLK, :].astype(f32)
        total = total.astype(bf16)
        for t in range(lat_count):
            r.d_cut[t, block * BLK : (block + 1) * BLK, :] = total[
                :, t * width : (t + 1) * width
            ]
    cut_copies = [
        begin(remote(r.d_cut.at[peer(k)], r.d_got.at[k - 1], {"lat": peer(k)}))
        for k in range(1, lat_count)
    ]
    for step in range(steps):
        for p in node_pieces:
            if step + 2 < steps:
                scatter_step(p, step + 2)
        for p in edge_pieces[::-1]:
            scatter_step(p, step)
    narrow = r.d_cut[lat].astype(f32)
    for k, copy in enumerate(cut_copies):
        copy.wait_recv()
        narrow = narrow + r.d_got[k].astype(f32)
    r.grad_nodes[...] = narrow.astype(bf16)
    for copy in out_copies:
        copy.wait_recv()
    for copy in sent:
        copy.wait_send()
    leave_latents()
    leave_grads()


def hand_out_kernel(*refs):
    sem = refs[-1]
    half = (len(refs) - 1) // 2
    copies = [
        pltpu.make_async_copy(refs[n], refs[half + n], sem.at[n]) for n in range(half)
    ]
    for copy in copies:
        copy.start()
    for copy in copies:
        copy.wait()


def hand_out(results):
    return pl.pallas_call(
        hand_out_kernel,
        out_shape=[jax.ShapeDtypeStruct(v.shape, v.dtype) for v in results],
        in_specs=[pl.BlockSpec(memory_space=pl.ANY)] * len(results),
        out_specs=[pl.BlockSpec(memory_space=pl.ANY)] * len(results),
        scratch_shapes=[pltpu.SemaphoreType.DMA((len(results),))],
        compiler_params=pltpu.CompilerParams(vmem_limit_bytes=60 * 1024 * 1024),
        name="hand_out",
    )(*results)


def per_device(
    nodes,
    edges,
    edge_tiles,
    edge_offsets,
    tile_counts,
    halo_blocks,
    w_edge_in,
    w_edge_out,
    w_node_in,
    w_node_out,
    edge_gain,
    node_gain,
    node_cotangent,
    edge_cotangent,
):
    slab_count, lat_count = lax.axis_size("slab"), lax.axis_size("lat")
    slab_bits, lat_bits = bits_of(slab_count), bits_of(lat_count)
    steps = slab_bits + lat_bits
    slab_rows, width = nodes.shape
    own_rows = slab_rows // lat_count
    halo_rows = HB * BLK
    all_rows = slab_rows + 2 * halo_rows
    edge_rows = edges.shape[0]
    bf16, f32 = jnp.bfloat16, jnp.float32
    weights = (w_edge_in, w_edge_out, w_node_in, w_node_out)
    whole_rows = [w.shape[0] * slab_count * lat_count for w in weights]
    vmem, smem = pl.BlockSpec(memory_space=pltpu.VMEM), pl.BlockSpec(memory_space=pltpu.SMEM)
    inputs = dict(
        nodes=nodes,
        edges=edges,
        edge_tiles=edge_tiles,
        edge_offsets=edge_offsets,
        tile_counts=tile_counts,
        halo_blocks=halo_blocks,
        w0=w_edge_in,
        w1=w_edge_out,
        w2=w_node_in,
        w3=w_node_out,
        edge_gain=edge_gain.reshape(1, -1),
        node_gain=node_gain.reshape(1, -1),
        node_cotangent=node_cotangent,
        edge_cotangent=edge_cotangent,
    )
    outputs = dict(
        new_nodes=((lat_count, own_rows, width), bf16),
        new_edges=(edges.shape, bf16),
        grad_nodes=(nodes.shape, bf16),
        grad_edges=(edges.shape, bf16),
        grad_out0=(w_edge_in.shape, f32),
        grad_out1=(w_edge_out.shape, f32),
        grad_out2=(w_node_in.shape, f32),
        grad_out3=(w_node_out.shape, f32),
    )
    scratch = dict(
        own=((lat_count, slab_rows, width), bf16),
        low=((lat_count, halo_rows, width), bf16),
        up=((lat_count, halo_rows, width), bf16),
        to_upper=((lat_count, halo_rows, width), bf16),
        to_lower=((lat_count, halo_rows, width), bf16),
        cot=((lat_count, own_rows, width), bf16),
        recv_hot=((slab_rows, edge_rows), bf16),
        send_hot=((all_rows, edge_rows), bf16),
        ext=((all_rows, L), bf16),
        joined=((3, edge_rows, L), bf16),
        recv_turned=((edge_rows, slab_rows), bf16),
        send_turned=((edge_rows, all_rows), bf16),
        joined_turned=((3, L, edge_rows), bf16),
        first_turned=((L, edge_rows), bf16),
        first=((edge_rows, L), bf16),
        normed=((edge_rows, L), f32),
        inverse=((edge_rows, 1), f32),
        top=((edge_rows, L), bf16),
        rest=((edge_rows, L), bf16),
        sums=((lat_count, own_rows, L), f32),
        sums_got=((lat_count - 1, own_rows, L), f32),
        d_agg=((lat_count, own_rows, L), bf16),
        rows_out=((lat_count, own_rows, width), bf16),
        d_edge=((edge_rows, L), bf16),
        d_ext=((all_rows, L), f32),
        d_cut=((lat_count, slab_rows, width), bf16),
        d_got=((lat_count - 1, slab_rows, width), bf16),
        back_low=((halo_rows, L), bf16),
        back_up=((halo_rows, L), bf16),
        from_below=((halo_rows, L), bf16),
        from_above=((halo_rows, L), bf16),
        mat0=((whole_rows[0], L), bf16),
        mat1=((whole_rows[1], L), bf16),
        mat2=((whole_rows[2], L), bf16),
        mat3=((whole_rows[3], L), bf16),
        wide=((max(whole_rows), L), f32),
    )
    names, shapes = list(scratch), list(scratch.values())
    for i in range(4):
        for _, rows, _ in pieces_of(weights[i].shape[0], GROUP_OF[i]):
            cut = (2,) * slab_bits + (lat_count, rows, L)
            names += [("full",), ("grad",)]
            shapes += [(cut, bf16)] * 2
            for k, shape in enumerate(sum_shapes(slab_bits, lat_count, rows, L)):
                names.append(("got",))
                shapes.append((shape, bf16))
                if k + 1 < steps:
                    names.append(("held",))
                    shapes.append((shape, bf16))
    count = names.count(("full",))
    copies = 2 * count * steps + 6 * (lat_count - 1) + 4
    results = pl.pallas_call(
        functools.partial(
            layer_kernel,
            slab_bits,
            lat_bits,
            [*inputs, *outputs, *names, "send_sem", "recv_sem"],
        ),
        out_shape=[jax.ShapeDtypeStruct(*o) for o in outputs.values()],
        in_specs=[smem if n in (2, 4, 5) else vmem for n in range(len(inputs))],
        out_specs=[vmem] * len(outputs),
        scratch_shapes=[pltpu.VMEM(*s) for s in shapes]
        + [pltpu.SemaphoreType.DMA((copies,)), pltpu.SemaphoreType.DMA((copies,))],
        compiler_params=pltpu.CompilerParams(
            collective_id=0, has_side_effects=True, vmem_limit_bytes=58 * 1024 * 1024
        ),
        name="mesh_layer",
    )(*inputs.values())
    return tuple(hand_out((results[0].reshape(nodes.shape), *results[1:])))


def solution(mesh):
    placed = (
        P("slab", "lat"),
        P(("slab", "lat"), None),
        P(None, ("slab", "lat")),
        P(None, ("slab", "lat")),
        P("slab"),
        P("slab", None, None),
        P(("slab", "lat"), None),
        P(("slab", "lat"), None),
        P(("slab", "lat"), None),
        P(("slab", "lat"), None),
        P(),
        P(),
        P("slab", "lat"),
        P(("slab", "lat"), None),
    )
    return jax.shard_map(
        per_device,
        mesh=mesh,
        in_specs=placed,
        out_specs=(
            P("slab", "lat"),
            P(("slab", "lat"), None),
            P("slab", "lat"),
            P(("slab", "lat"), None),
            P(("slab", "lat"), None),
            P(("slab", "lat"), None),
            P(("slab", "lat"), None),
            P(("slab", "lat"), None),
        ),
        check_vma=False,
    )
```
